128 devices in a mesh: tm: 16 (over z, x_lo, core), inp: 8 (over y, x_hi).
Axes of the slice: x: 4 (x_hi: 2, x_lo: 2; x = x_hi * 2 + x_lo), y: 4, z: 4, core: 2. Of those that a mesh axis runs over, the one named last changes fastest.
Arguments:
- voltages: bfloat16 [512, 2097152], P('inp', 'tm'), may hold values from -6 to 6
- taps: float32 [8, 16384], replicated, may hold values from -2 to 2
Outputs:
- visibility: float32 [512, 2, 512, 512], P(('tm', 'inp'))
The draws below stay inside these ranges and needn't reach their ends.
All inputs are finite; a program needn't handle non-finite values.
Results may differ from the reference program's by a relative error of at most 0.0059.
Values may be sent and summed in bfloat16 or wider, within the bound.
No kernel may reach another device: no remote copies, remote signals or barrier semaphores. Data moves between devices by JAX's collectives and lax.ppermute only.
A program may use at most 256 MiB of HBM per device.

```python
import math
import jax
import jax.numpy as jnp
from jax import lax

INPUTS = 512
LEN = 16384
CH = 512
TAPS = 8
START = 1024
FRAMES = 128


def block_scale(key, extent, split, least, largest):
    factor_of, own = 1.0, jax.random.fold_in(key, 6)
    for position, blocks in split:
        heights = jnp.exp(jax.random.uniform(jax.random.fold_in(own, position), (blocks,), jnp.float32, least / len(split), largest / len(split)))
        factor_of = factor_of * jnp.repeat(heights, extent[position] // blocks).reshape([-1 if axis == position else 1 for axis in range(len(extent))])
    return factor_of


def noise(own_key, extent, spread, reach, cuts=(), kind=jnp.bfloat16):
    entries = jax.random.normal(own_key, extent, jnp.float32) * spread
    if len(cuts) > 0:
        entries = block_scale(own_key, extent, cuts, -0.22, 0.18) * entries
    return jnp.clip(entries, min=-reach, max=reach).astype(kind)


def setup_inputs(seed: int = 0) -> dict:
    splits = jax.random.split(jax.random.key(seed), 3)
    return {
        "voltages": noise(splits[0], (INPUTS, FRAMES * LEN), 1.0, 6.0, ((0, 8), (1, 16))),
        "taps": noise(splits[1], (TAPS, LEN), TAPS ** -0.5, 2.0, (), jnp.float32),
    }


def dft_table(frame_len, first, count):
    rows_idx = jnp.arange(frame_len, dtype=jnp.int32)[:, None]
    cols_idx = (jnp.arange(count, dtype=jnp.int32) + first)[None, :]
    phase = rows_idx * cols_idx % frame_len
    angle = phase.astype(jnp.float32) * jnp.float32(2.0 * math.pi / frame_len)
    return jnp.concatenate([jnp.cos(angle), -jnp.sin(angle)], axis=1).astype(jnp.bfloat16)

def reference(voltages, taps):
    blocks = voltages.reshape(INPUTS, FRAMES, LEN)
    padded = jnp.concatenate([jnp.zeros((INPUTS, TAPS - 1, LEN), jnp.bfloat16), blocks], axis=1)
    table = dft_table(LEN, START, CH).astype(jnp.float32)
    reversed_taps = taps[::-1].astype(jnp.float32)
    scale = jnp.float32(1.0 / math.sqrt(LEN))

    def one_frame(frame):
        window = lax.dynamic_slice(padded, (jnp.int32(0), frame.astype(jnp.int32), jnp.int32(0)), (INPUTS, TAPS, LEN))
        filtered = lax.optimization_barrier(jnp.sum(window.astype(jnp.float32) * reversed_taps[None, :, :], axis=1)).astype(jnp.bfloat16)
        spectra = jnp.dot(filtered.astype(jnp.float32), table, preferred_element_type=jnp.float32)
        return (spectra * scale).astype(jnp.bfloat16)
    spectra = lax.map(one_frame, jnp.arange(FRAMES, dtype=jnp.int32))
    cube = spectra.reshape(FRAMES, INPUTS, 2, CH)
    cube = jnp.transpose(cube, (3, 2, 1, 0)).reshape(CH, 2 * INPUTS, FRAMES)

    def one_channel(stacked):
        stacked = stacked.astype(jnp.float32)
        product = jnp.dot(stacked, stacked.T, preferred_element_type=jnp.float32)
        real_part = product[:INPUTS, :INPUTS] + product[INPUTS:, INPUTS:]
        imag_part = product[INPUTS:, :INPUTS] - product[:INPUTS, INPUTS:]
        return jnp.stack([real_part, imag_part]) / jnp.float32(FRAMES)
    return lax.map(one_channel, cube)
```

```python
import functools
import math

import jax
import jax.numpy as jnp
from jax import lax
from jax.experimental import pallas as pl
from jax.experimental.pallas import tpu as pltpu
from jax.sharding import PartitionSpec as P

CH = 512
START = 1024
RADIX = 4
LANES = 128
NT = (((1,), (1,)), ((), ()))
TN = (((0,), (0,)), ((), ()))
PLACES = ((0, 1), (4, 6), (2, 3), (7, 5))


def unit_roots(phase, frame_len):
    angle = (phase % frame_len).astype(jnp.float32) * jnp.float32(2.0 * math.pi / frame_len)
    return jnp.cos(angle), jnp.sin(angle)


def table_kernel(groups, step_cos, step_sin, first_cos, first_sin, coarse_cos, coarse_sin, out, fine_cos, fine_sin):
    quarter = step_cos.shape[0]

    @pl.when(pl.program_id(0) == 0)
    def _():
        for res in range(RADIX):
            c0, s0 = step_cos[...], step_sin[...]
            c1, s1 = first_cos[res : res + 1, :], first_sin[res : res + 1, :]
            fine_cos[res] = c0 * c1 - s0 * s1
            fine_sin[res] = s0 * c1 + c0 * s1

    for group in range(groups):
        lanes = slice(group * LANES, (group + 1) * LANES)
        for res in range(RADIX):
            rows = slice(res * quarter, (res + 1) * quarter)
            c0, s0 = fine_cos[res], fine_sin[res]
            c1, s1 = coarse_cos[0, rows, group : group + 1], coarse_sin[0, rows, group : group + 1]
            cosine, sine = PLACES[res]
            out[cosine * quarter : (cosine + 1) * quarter, lanes] = (c0 * c1 - s0 * s1).astype(jnp.bfloat16)
            out[sine * quarter : (sine + 1) * quarter, lanes] = (-s0 * c1 - c0 * s1).astype(jnp.bfloat16)


def twiddles(frame_len, groups=4):
    span = frame_len // RADIX
    quarter = CH // RADIX
    steps = span // (LANES * groups)
    columns = jnp.arange(LANES, dtype=jnp.int32)[None, :]
    offsets = jnp.arange(quarter, dtype=jnp.int32)[:, None]
    step = unit_roots(RADIX * offsets * columns, frame_len)
    first = unit_roots((START + jnp.arange(8, dtype=jnp.int32)[:, None]) * columns, frame_len)
    channels = START + jnp.arange(RADIX, dtype=jnp.int32)[:, None, None] + RADIX * offsets[None]
    blocks = LANES * jnp.arange(span // LANES, dtype=jnp.int32)
    coarse = unit_roots(channels.reshape(CH, 1) * blocks[None, :], frame_len)
    coarse = lax.optimization_barrier(coarse)
    coarse = [jnp.transpose(part.reshape(CH, steps, groups), (1, 0, 2)) for part in coarse]
    return pl.pallas_call(
        functools.partial(table_kernel, groups),
        grid=(steps,),
        in_specs=[pl.BlockSpec((quarter, LANES), lambda i: (0, 0))] * 2
        + [pl.BlockSpec((8, LANES), lambda i: (0, 0))] * 2
        + [pl.BlockSpec((1, CH, groups), lambda i: (i, 0, 0))] * 2,
        out_specs=pl.BlockSpec((2 * CH, groups * LANES), lambda i: (0, i)),
        out_shape=jax.ShapeDtypeStruct((2 * CH, span), jnp.bfloat16),
        scratch_shapes=[pltpu.VMEM((RADIX, quarter, LANES), jnp.float32)] * 2,
        name="twiddles",
    )(*step, *first, *coarse)


def spectra_kernel(tail, frames, width, samples, taps, table, out, parts, sums_ref, stage):
    step = pl.program_id(0)
    taps_count = taps.shape[1]
    groups, low = samples.shape[0], samples.shape[2]
    in_dev = groups * low
    made = taps_count - 1 if tail else frames
    columns = frames * in_dev

    @pl.when(step == 0)
    def _():
        sums_ref[...] = jnp.zeros_like(sums_ref)
        if tail:
            parts[...] = jnp.zeros_like(parts)

    for lane in range(width // LANES):
        lanes = slice(lane * LANES, (lane + 1) * LANES)
        for group in range(groups):
            block = [
                [samples[group, n * RADIX + b, :, lanes].astype(jnp.float32) for n in range(frames)]
                for b in range(RADIX)
            ]
            for m in range(made):
                quad = []
                for b in range(RADIX):
                    total = None
                    for t in range(taps_count):
                        n = frames + m - t if tail else m - t
                        if 0 <= n < frames:
                            term = taps[b, t : t + 1, lanes] * block[b][n]
                            total = term if total is None else total + term
                    quad.append(total)
                s02, d02 = quad[0] + quad[2], quad[0] - quad[2]
                s13, d13 = quad[1] + quad[3], quad[1] - quad[3]
                start = m * in_dev + group * low
                rows = slice(start, start + low)
                parts[0, rows, lanes] = s02 + s13
                parts[1, rows, lanes] = s02 - s13
                parts[2, rows, lanes] = d02
                parts[3, rows, lanes] = d13

    quarter = table.shape[0] // (2 * RADIX)

    def product(block, part, negative=False):
        rows = table[2 * block * quarter : 2 * (block + 1) * quarter, :]
        rows = -rows if negative else rows
        return lax.dot_general(rows, parts[part], NT, preferred_element_type=jnp.float32)

    sums_ref[0] += product(0, 0)
    sums_ref[1] += product(1, 1)
    sums_ref[2] += product(2, 2) + product(3, 3)
    sums_ref[3] += product(3, 2) + product(2, 3, True)

    @pl.when(step == pl.num_programs(0) - 1)
    def _():
        scale = jnp.float32(1.0 / math.sqrt(RADIX * width * pl.num_programs(0)))
        tiles = columns // LANES
        height = 2 * RADIX * tiles
        target = stage if tail else out
        for place, (block, part) in enumerate(((0, 0), (0, 1), (2, 0), (3, 0), (1, 0), (1, 1), (3, 1), (2, 1))):
            for tile in range(tiles):
                target[pl.ds(place * tiles + tile, quarter, stride=height), :] = (
                    sums_ref[block, part * quarter : (part + 1) * quarter, tile * LANES : (tile + 1) * LANES]
                    * scale
                )
        if tail:
            out[...] = stage[...].astype(out.dtype)


def frame_spectra(voltages, taps, table, tail, width=512):
    in_dev, length = voltages.shape
    tap_count, frame_len = taps.shape
    frames = length // frame_len
    span = frame_len // RADIX
    quarter = CH // RADIX
    columns = frames * in_dev

    low = 8
    samples = voltages.reshape(in_dev // low, low, frames * RADIX, span)
    samples = jnp.transpose(samples, (0, 2, 1, 3))
    taps = jnp.transpose(taps.reshape(tap_count, RADIX, span), (1, 0, 2))
    in_specs = [
        pl.BlockSpec((in_dev // low, frames * RADIX, low, width), lambda i: (0, 0, 0, i)),
        pl.BlockSpec((RADIX, tap_count, width), lambda i: (0, 0, i)),
        pl.BlockSpec((2 * CH, width), lambda i: (0, i)),
    ]
    height = quarter * 2 * RADIX * (columns // LANES)
    return pl.pallas_call(
        functools.partial(spectra_kernel, tail, frames, width),
        grid=(span // width,),
        in_specs=in_specs,
        out_specs=pl.BlockSpec((height, LANES), lambda i: (0, 0)),
        out_shape=jax.ShapeDtypeStruct((height, LANES), jnp.bfloat16 if tail else jnp.float32),
        scratch_shapes=[
            pltpu.VMEM((RADIX, columns, width), jnp.float32),
            pltpu.VMEM((RADIX, 2 * quarter, columns), jnp.float32),
            pltpu.VMEM((height if tail else 8, LANES), jnp.float32),
        ],
        compiler_params=pltpu.CompilerParams(vmem_limit_bytes=50 * 2**20),
        cost_estimate=pl.CostEstimate(
            flops=2 * columns * 6 * quarter * 2 * span, bytes_accessed=26 * 2**20, transcendentals=0
        ),
        name="tail_spectra" if tail else "main_spectra",
    )(samples, taps, table)


def visibility_kernel(tm_count, inp_count, total_frames, block, out, left, right):
    lane = lax.broadcasted_iota(jnp.int32, (tm_count, 8, LANES), 2)
    row = lax.broadcasted_iota(jnp.int32, (tm_count, 8, LANES), 1)
    low = lane < LANES // 2
    real_row = row < 4
    half_depth = tm_count * 8
    scale = jnp.float32(1.0 / total_frames)
    for channel in range(block.shape[1] // 8):
        values = block[...].astype(jnp.float32)[:, channel * 8 : channel * 8 + 8, :]
        values = values.reshape(tm_count, inp_count, 8, LANES)
        for pair in range(inp_count // 2):
            first, second = values[:, 2 * pair], values[:, 2 * pair + 1]
            merged = (
                jnp.where(low, first, pltpu.roll(second, LANES // 2, 2)),
                jnp.where(low, pltpu.roll(first, LANES // 2, 2), second),
            )
            lanes = slice(pair * LANES, (pair + 1) * LANES)
            for part in range(2):
                rows = slice(part * half_depth, (part + 1) * half_depth)
                swapped = pltpu.roll(merged[part], 4, 1)
                swapped = jnp.where(real_row, -swapped, swapped)
                left[rows, lanes] = merged[part].reshape(half_depth, LANES).astype(jnp.bfloat16)
                right[rows, lanes] = swapped.reshape(half_depth, LANES).astype(jnp.bfloat16)
        out[channel, 0] = (
            lax.dot_general(left[...], left[...], TN, preferred_element_type=jnp.float32) * scale
        )
        out[channel, 1] = (
            lax.dot_general(left[...], right[...], TN, preferred_element_type=jnp.float32) * scale
        )


def visibilities(spectra, tm_count, inp_count, total_frames, inputs_all):
    devices, height, _ = spectra.shape
    per_device = CH // devices
    depth = 2 * tm_count * 8
    return pl.pallas_call(
        functools.partial(visibility_kernel, tm_count, inp_count, total_frames),
        grid=(height // 16,),
        in_specs=[pl.BlockSpec((devices, 16, LANES), lambda i: (0, i, 0))],
        out_specs=pl.BlockSpec((2, 2, inputs_all, inputs_all), lambda i: (i, 0, 0, 0)),
        out_shape=jax.ShapeDtypeStruct((per_device, 2, inputs_all, inputs_all), jnp.float32),
        scratch_shapes=[
            pltpu.VMEM((depth, inputs_all), jnp.bfloat16),
            pltpu.VMEM((depth, inputs_all), jnp.bfloat16),
        ],
        compiler_params=pltpu.CompilerParams(vmem_limit_bytes=50 * 2**20),
        name="visibilities",
    )(spectra)


def on_device(voltages, taps):
    in_dev, samples = voltages.shape
    frame_len = taps.shape[1]
    frames_dev = samples // frame_len
    tm_count, inp_count = lax.axis_size("tm"), lax.axis_size("inp")
    devices = tm_count * inp_count
    table = twiddles(frame_len)
    tail = frame_spectra(voltages, taps, table, True)
    tail, table, voltages = lax.optimization_barrier((tail, table, voltages))
    carried = lax.ppermute(tail, "tm", [(i, i + 1) for i in range(tm_count - 1)])
    main = frame_spectra(voltages, taps, table, False)
    spectra = (main + carried.astype(jnp.float32)).astype(jnp.bfloat16)
    spectra = spectra.reshape(devices, -1, LANES)
    spectra = lax.all_to_all(spectra, ("tm", "inp"), split_axis=0, concat_axis=0, tiled=True)
    return visibilities(spectra, tm_count, inp_count, tm_count * frames_dev, inp_count * in_dev)


def solution(mesh):
    return jax.shard_map(
        on_device,
        mesh=mesh,
        in_specs=(P("inp", "tm"), P()),
        out_specs=P(("tm", "inp"), None, None, None),
        check_vma=False,
    )
```

```python
import functools
import math

import jax
import jax.numpy as jnp
from jax import lax
from jax.experimental import pallas as pl
from jax.experimental.pallas import tpu as pltpu
from jax.sharding import PartitionSpec as P

CH = 512
START = 1024
RADIX = 4
LANES = 128
NT = (((1,), (1,)), ((), ()))
TN = (((0,), (0,)), ((), ()))
PLACES = ((0, 1), (4, 6), (2, 3), (7, 5))


def unit_roots(phase, frame_len):
    angle = (phase % frame_len).astype(jnp.float32) * jnp.float32(2.0 * math.pi / frame_len)
    return jnp.cos(angle), -jnp.sin(angle)


def turned(first, second):
    return first[0] * second[0] - first[1] * second[1], first[1] * second[0] + first[0] * second[1]


def table_kernel(frame_len, out):
    _, rows, span = out.shape
    shape = (rows, LANES)
    channel = pl.program_id(0) * rows + lax.broadcasted_iota(jnp.int32, shape, 0)
    column = lax.broadcasted_iota(jnp.int32, shape, 1)
    fine = unit_roots(RADIX * channel * column, frame_len)
    advance = unit_roots(RADIX * LANES * channel, frame_len)
    residue = lax.broadcasted_iota(jnp.int32, (8, LANES), 0)
    base = unit_roots((START + residue) * lax.broadcasted_iota(jnp.int32, (8, LANES), 1), frame_len)
    for res in range(RADIX):
        value = turned(fine, tuple(part[res : res + 1, :] for part in base))
        angle = 2.0 * math.pi * (LANES * (START + res) % frame_len) / frame_len
        turn = turned(advance, (jnp.float32(math.cos(angle)), jnp.float32(-math.sin(angle))))
        cosine, sine = PLACES[res]
        for start in range(0, span, LANES):
            out[cosine, :, start : start + LANES] = value[0].astype(jnp.bfloat16)
            out[sine, :, start : start + LANES] = value[1].astype(jnp.bfloat16)
            value = turned(value, turn)


def twiddles(frame_len):
    span = frame_len // RADIX
    quarter = CH // RADIX
    rows = 16
    table = pl.pallas_call(
        functools.partial(table_kernel, frame_len),
        grid=(quarter // rows,),
        out_specs=pl.BlockSpec((2 * RADIX, rows, span), lambda i: (0, i, 0)),
        out_shape=jax.ShapeDtypeStruct((2 * RADIX, quarter, span), jnp.bfloat16),
        name="twiddles",
    )()
    return table.reshape(2 * CH, span)


def spectra_kernel(tail, frames, width, batch, samples, taps, table, out, parts, sums_ref, wide):
    step = pl.program_id(0)
    taps_count = taps.shape[1]
    groups, low = samples.shape[0], samples.shape[2]
    in_dev = groups * low
    made = taps_count - 1 if tail else frames
    columns = frames * in_dev

    @pl.when(step == 0)
    def _():
        sums_ref[...] = jnp.zeros_like(sums_ref)
        if tail:
            parts[...] = jnp.zeros_like(parts)

    base = step % batch * width
    for lane in range(width // LANES):
        lanes = slice(lane * LANES, (lane + 1) * LANES)
        places = pl.ds(pl.multiple_of(base + lane * LANES, LANES), LANES)
        for b in range(RADIX):
            for t in range(taps_count):
                wide[lane % 2, b, t] = jnp.broadcast_to(taps[b, t : t + 1, lanes], (low, LANES))
        for group in range(groups):
            sums = []
            for b in (0, 2, 1, 3):
                block = [samples[group, n * RADIX + b, :, lanes].astype(jnp.float32) for n in range(frames)]
                totals = [None] * made
                for t in range(taps_count):
                    weight = wide[lane % 2, b, t]
                    for m in range(made):
                        n = frames + m - t if tail else m - t
                        if 0 <= n < frames:
                            term = weight * block[n]
                            totals[m] = term if totals[m] is None else totals[m] + term
                sums.append(totals)
                if b < 2:
                    continue
                second, first = sums.pop(), sums.pop()
                for m in range(made):
                    rows = slice(m * in_dev + group * low, m * in_dev + (group + 1) * low)
                    parts[b, rows, places] = first[m] - second[m]
                    first[m] = first[m] + second[m]
                    if b == 3:
                        parts[0, rows, places] = sums[0][m] + first[m]
                        parts[1, rows, places] = sums[0][m] - first[m]
                sums.append(first)

    quarter = table.shape[0] // (2 * RADIX)

    def product(block, part, negative=False):
        rows = table[2 * block * quarter : 2 * (block + 1) * quarter, :]
        rows = -rows if negative else rows
        return lax.dot_general(rows, parts[part], NT, preferred_element_type=jnp.float32)

    @pl.when(step % batch == batch - 1)
    def _():
        sums_ref[0] += product(0, 0)
        sums_ref[1] += product(1, 1)
        sums_ref[2] += product(2, 2) + product(3, 3)
        sums_ref[3] += product(3, 2) + product(2, 3, True)

    @pl.when(step == pl.num_programs(0) - 1)
    def _():
        scale = jnp.float32(1.0 / math.sqrt(RADIX * width * pl.num_programs(0)))
        tiles = columns // LANES
        height = 2 * RADIX * tiles
        order = ((0, 0), (0, 1), (2, 0), (3, 0), (1, 0), (1, 1), (3, 1), (2, 1))
        for start in range(0, quarter, 8):
            pieces = [
                sums_ref[block, part * quarter + start : part * quarter + start + 8, tile * LANES : (tile + 1) * LANES]
                for block, part in order
                for tile in range(tiles)
            ]
            value = jnp.transpose(jnp.stack(pieces), (1, 0, 2)) * scale
            out[start : start + 8] = value.astype(out.dtype)


def frame_spectra(voltages, taps, table, tail, width=512, batch=2):
    in_dev, length = voltages.shape
    tap_count, frame_len = taps.shape
    frames = length // frame_len
    span = frame_len // RADIX
    quarter = CH // RADIX
    columns = frames * in_dev

    low = 8
    samples = voltages.reshape(in_dev // low, low, frames * RADIX, span)
    samples = jnp.transpose(samples, (0, 2, 1, 3))
    taps = jnp.transpose(taps.reshape(tap_count, RADIX, span), (1, 0, 2))
    in_specs = [
        pl.BlockSpec((in_dev // low, frames * RADIX, low, width), lambda i: (0, 0, 0, i)),
        pl.BlockSpec((RADIX, tap_count, width), lambda i: (0, 0, i)),
        pl.BlockSpec((2 * CH, batch * width), lambda i: (0, i // batch)),
    ]
    height = 2 * RADIX * (columns // LANES)
    return pl.pallas_call(
        functools.partial(spectra_kernel, tail, frames, width, batch),
        grid=(span // width,),
        in_specs=in_specs,
        out_specs=pl.BlockSpec((quarter, height, LANES), lambda i: (0, 0, 0)),
        out_shape=jax.ShapeDtypeStruct((quarter, height, LANES), jnp.bfloat16 if tail else jnp.float32),
        scratch_shapes=[
            pltpu.VMEM((RADIX, columns, batch * width), jnp.float32),
            pltpu.VMEM((RADIX, 2 * quarter, columns), jnp.float32),
            pltpu.VMEM((2, RADIX, tap_count, low, LANES), jnp.float32),
        ],
        compiler_params=pltpu.CompilerParams(vmem_limit_bytes=50 * 2**20),
        cost_estimate=pl.CostEstimate(
            flops=2 * columns * 6 * quarter * 2 * span, bytes_accessed=26 * 2**20, transcendentals=0
        ),
        name="tail_spectra" if tail else "main_spectra",
    )(samples, taps, table)


def visibility_kernel(tm_count, inp_count, total_frames, block, out, left, right):
    lane = lax.broadcasted_iota(jnp.int32, (tm_count, 8, LANES), 2)
    row = lax.broadcasted_iota(jnp.int32, (tm_count, 8, LANES), 1)
    low = lane < LANES // 2
    real_row = row < 4
    half_depth = tm_count * 8
    scale = jnp.float32(1.0 / total_frames)
    for channel in range(block.shape[1] // 8):
        values = block[...].astype(jnp.float32)[:, channel * 8 : channel * 8 + 8, :]
        values = values.reshape(tm_count, inp_count, 8, LANES)
        for pair in range(inp_count // 2):
            first, second = values[:, 2 * pair], values[:, 2 * pair + 1]
            merged = (
                jnp.where(low, first, pltpu.roll(second, LANES // 2, 2)),
                jnp.where(low, pltpu.roll(first, LANES // 2, 2), second),
            )
            lanes = slice(pair * LANES, (pair + 1) * LANES)
            for part in range(2):
                rows = slice(part * half_depth, (part + 1) * half_depth)
                swapped = pltpu.roll(merged[part], 4, 1)
                swapped = jnp.where(real_row, -swapped, swapped)
                left[rows, lanes] = merged[part].reshape(half_depth, LANES).astype(jnp.bfloat16)
                right[rows, lanes] = swapped.reshape(half_depth, LANES).astype(jnp.bfloat16)
        out[channel, 0] = (
            lax.dot_general(left[...], left[...], TN, preferred_element_type=jnp.float32) * scale
        )
        out[channel, 1] = (
            lax.dot_general(left[...], right[...], TN, preferred_element_type=jnp.float32) * scale
        )


def visibilities(spectra, tm_count, inp_count, total_frames, inputs_all):
    devices, height, _ = spectra.shape
    per_device = CH // devices
    depth = 2 * tm_count * 8
    return pl.pallas_call(
        functools.partial(visibility_kernel, tm_count, inp_count, total_frames),
        grid=(height // 16,),
        in_specs=[pl.BlockSpec((devices, 16, LANES), lambda i: (0, i, 0))],
        out_specs=pl.BlockSpec((2, 2, inputs_all, inputs_all), lambda i: (i, 0, 0, 0)),
        out_shape=jax.ShapeDtypeStruct((per_device, 2, inputs_all, inputs_all), jnp.float32),
        scratch_shapes=[
            pltpu.VMEM((depth, inputs_all), jnp.bfloat16),
            pltpu.VMEM((depth, inputs_all), jnp.bfloat16),
        ],
        compiler_params=pltpu.CompilerParams(vmem_limit_bytes=50 * 2**20),
        name="visibilities",
    )(spectra)


def on_device(voltages, taps):
    in_dev, samples = voltages.shape
    frame_len = taps.shape[1]
    frames_dev = samples // frame_len
    tm_count, inp_count = lax.axis_size("tm"), lax.axis_size("inp")
    devices = tm_count * inp_count
    table = twiddles(frame_len)
    tail = frame_spectra(voltages, taps, table, True)
    tail, table, voltages = lax.optimization_barrier((tail, table, voltages))
    carried = lax.ppermute(tail, "tm", [(i, i + 1) for i in range(tm_count - 1)])
    main = frame_spectra(voltages, taps, table, False)
    spectra = (main + carried.astype(jnp.float32)).astype(jnp.bfloat16)
    spectra = spectra.reshape(devices, -1, LANES)
    spectra = lax.all_to_all(spectra, ("tm", "inp"), split_axis=0, concat_axis=0, tiled=True)
    return visibilities(spectra, tm_count, inp_count, tm_count * frames_dev, inp_count * in_dev)


def solution(mesh):
    return jax.shard_map(
        on_device,
        mesh=mesh,
        in_specs=(P("inp", "tm"), P()),
        out_specs=P(("tm", "inp"), None, None, None),
        check_vma=False,
    )
```

```python
import functools
import math

import jax
import jax.numpy as jnp
from jax import lax
from jax.experimental import pallas as pl
from jax.experimental.pallas import tpu as pltpu
from jax.sharding import PartitionSpec as P

CH = 512
START = 1024
RADIX = 8
LANES = 128
NT = (((1,), (1,)), ((), ()))
TN = (((0,), (0,)), ((), ()))
PAIRS = ((1, 7), (2, 6), (3, 5))
TABLE_PARTS = 4 + 6 * len(PAIRS)
EVEN_ORDER = (0, 1, 4, 6, 8, 10, 12, 14)
ODD_ORDER = (2, 3, 15, 13, 11, 9, 7, 5)


def unit_roots(phase, frame_len):
    angle = (phase % frame_len).astype(jnp.float32) * jnp.float32(2.0 * math.pi / frame_len)
    return jnp.cos(angle), -jnp.sin(angle)


def turned(first, second):
    return first[0] * second[0] - first[1] * second[1], first[1] * second[0] + first[0] * second[1]


def table_places(res):
    if res % 4 == 0:
        return ((res // 2, False),), ((res // 2 + 1, False),)
    for index, (lead, mirror) in enumerate(PAIRS):
        start = 4 + 6 * index
        if res == lead:
            return ((start, False), (start + 4, True)), ((start + 2, False),)
        if res == mirror:
            return ((start + 3, False),), ((start + 1, False), (start + 5, True))


def table_kernel(frame_len, out):
    _, rows, span = out.shape
    shape = (rows, LANES)
    channel = pl.program_id(0) * rows + lax.broadcasted_iota(jnp.int32, shape, 0)
    column = lax.broadcasted_iota(jnp.int32, shape, 1)
    fine = unit_roots(RADIX * channel * column, frame_len)
    advance = unit_roots(RADIX * LANES * channel, frame_len)
    residue = lax.broadcasted_iota(jnp.int32, (RADIX, LANES), 0)
    base = unit_roots((START + residue) * lax.broadcasted_iota(jnp.int32, (RADIX, LANES), 1), frame_len)
    for res in range(RADIX):
        value = turned(fine, tuple(part[res : res + 1, :] for part in base))
        angle = 2.0 * math.pi * (LANES * (START + res) % frame_len) / frame_len
        turn = turned(advance, (jnp.float32(math.cos(angle)), jnp.float32(-math.sin(angle))))
        places = table_places(res)
        for start in range(0, span, LANES):
            for which in range(2):
                entry = value[which].astype(jnp.bfloat16)
                for part, negated in places[which]:
                    out[part, :, start : start + LANES] = -entry if negated else entry
            value = turned(value, turn)


def twiddles(frame_len):
    span = frame_len // RADIX
    eighth = CH // RADIX
    rows = 16
    table = pl.pallas_call(
        functools.partial(table_kernel, frame_len),
        grid=(eighth // rows,),
        out_specs=pl.BlockSpec((TABLE_PARTS, rows, span), lambda i: (0, i, 0)),
        out_shape=jax.ShapeDtypeStruct((TABLE_PARTS, eighth, span), jnp.bfloat16),
        name="twiddles",
    )()
    return table.reshape(TABLE_PARTS * eighth, span)


def spectra_kernel(tail, frames, width, batch, samples, taps, table, out, parts, sums_ref, wide):
    step = pl.program_id(0)
    taps_count = taps.shape[1]
    groups, low = samples.shape[0], samples.shape[2]
    in_dev = groups * low
    made = taps_count - 1 if tail else frames
    columns = frames * in_dev

    @pl.when(step == 0)
    def _():
        sums_ref[...] = jnp.zeros_like(sums_ref)
        if tail:
            parts[...] = jnp.zeros_like(parts)

    base = step % batch * width
    for lane in range(width // LANES):
        lanes = slice(lane * LANES, (lane + 1) * LANES)
        places = pl.ds(pl.multiple_of(base + lane * LANES, LANES), LANES)
        for b in range(RADIX):
            for t in range(taps_count):
                wide[lane % 2, b, t] = jnp.broadcast_to(taps[b, t : t + 1, lanes], (low, LANES))
        for group in range(groups):
            kept = []
            for first in (0, 2, 1, 3):
                pair = []
                for b in (first, first + 4):
                    block = [samples[group, n * RADIX + b, :, lanes].astype(jnp.float32) for n in range(frames)]
                    totals = [None] * made
                    for t in range(taps_count):
                        weight = wide[lane % 2, b, t]
                        for m in range(made):
                            n = frames + m - t if tail else m - t
                            if 0 <= n < frames:
                                term = weight * block[n]
                                totals[m] = term if totals[m] is None else totals[m] + term
                    pair.append(totals)
                kept.append(([x + y for x, y in zip(*pair)], [x - y for x, y in zip(*pair)]))
            (s0, d0), (s2, d2), (s1, d1), (s3, d3) = kept
            root = jnp.float32(math.sqrt(0.5))
            for m in range(made):
                rows = slice(m * in_dev + group * low, m * in_dev + (group + 1) * low)
                even, odd = s0[m] + s2[m], s1[m] + s3[m]
                across, along = (d1[m] - d3[m]) * root, (d1[m] + d3[m]) * root
                parts[0, rows, places] = even + odd
                parts[1, rows, places] = even - odd
                parts[2, rows, places] = d0[m] + across
                parts[3, rows, places] = along + d2[m]
                parts[4, rows, places] = s0[m] - s2[m]
                parts[5, rows, places] = s1[m] - s3[m]
                parts[6, rows, places] = d0[m] - across
                parts[7, rows, places] = along - d2[m]

    eighth = table.shape[0] // TABLE_PARTS

    def product(first, last, part):
        rows = table[first * eighth : last * eighth, :]
        return lax.dot_general(rows, parts[part], NT, preferred_element_type=jnp.float32)

    @pl.when(step % batch == batch - 1)
    def _():
        sums_ref[: 2 * eighth] += product(0, 2, 0)
        sums_ref[2 * eighth : 4 * eighth] += product(2, 4, 1)
        for index in range(len(PAIRS)):
            rows = slice((4 + 4 * index) * eighth, (8 + 4 * index) * eighth)
            first = 4 + 6 * index
            sums_ref[rows] += product(first, first + 4, 2 + 2 * index) + product(first + 2, first + 6, 3 + 2 * index)

    @pl.when(step == pl.num_programs(0) - 1)
    def _():
        scale = jnp.float32(1.0 / math.sqrt(RADIX * width * pl.num_programs(0)))
        tiles = columns // LANES
        height = 2 * RADIX * tiles
        for start in range(0, eighth, 8):
            both = []
            for order in (EVEN_ORDER, ODD_ORDER):
                pieces = [
                    sums_ref[part * eighth + start : part * eighth + start + 8, tile * LANES : (tile + 1) * LANES]
                    for part in order
                    for tile in range(tiles)
                ]
                both.append(jnp.transpose(jnp.stack(pieces), (1, 0, 2)) * scale)
            value = jnp.stack(both, axis=1).reshape(16, len(pieces), LANES)
            out[2 * start : 2 * start + 16] = value.astype(out.dtype)


def frame_spectra(voltages, taps, table, tail, width=256, batch=4):
    in_dev, length = voltages.shape
    tap_count, frame_len = taps.shape
    frames = length // frame_len
    span = frame_len // RADIX
    devices = CH // 4
    columns = frames * in_dev

    low = 8
    samples = voltages.reshape(in_dev // low, low, frames * RADIX, span)
    samples = jnp.transpose(samples, (0, 2, 1, 3))
    taps = jnp.transpose(taps.reshape(tap_count, RADIX, span), (1, 0, 2))
    in_specs = [
        pl.BlockSpec((in_dev // low, frames * RADIX, low, width), lambda i: (0, 0, 0, i)),
        pl.BlockSpec((RADIX, tap_count, width), lambda i: (0, 0, i)),
        pl.BlockSpec((table.shape[0], batch * width), lambda i: (0, i // batch)),
    ]
    height = 8 * (columns // LANES)
    return pl.pallas_call(
        functools.partial(spectra_kernel, tail, frames, width, batch),
        grid=(span // width,),
        in_specs=in_specs,
        out_specs=pl.BlockSpec((devices, height, LANES), lambda i: (0, 0, 0)),
        out_shape=jax.ShapeDtypeStruct((devices, height, LANES), jnp.bfloat16 if tail else jnp.float32),
        scratch_shapes=[
            pltpu.VMEM((RADIX, columns, batch * width), jnp.float32),
            pltpu.VMEM((2 * CH, columns), jnp.float32),
            pltpu.VMEM((2, RADIX, tap_count, low, LANES), jnp.float32),
        ],
        compiler_params=pltpu.CompilerParams(vmem_limit_bytes=50 * 2**20),
        cost_estimate=pl.CostEstimate(
            flops=2 * columns * (7 * CH // 2) * span, bytes_accessed=26 * 2**20, transcendentals=0
        ),
        name="tail_spectra" if tail else "main_spectra",
    )(samples, taps, table)


def visibility_kernel(tm_count, inp_count, total_frames, block, out, left, right):
    lane = lax.broadcasted_iota(jnp.int32, (tm_count, 8, LANES), 2)
    row = lax.broadcasted_iota(jnp.int32, (tm_count, 8, LANES), 1)
    low = lane < LANES // 2
    real_row = row < 4
    half_depth = tm_count * 8
    scale = jnp.float32(1.0 / total_frames)
    for channel in range(block.shape[1] // 8):
        values = block[...].astype(jnp.float32)[:, channel * 8 : channel * 8 + 8, :]
        values = values.reshape(tm_count, inp_count, 8, LANES)
        for pair in range(inp_count // 2):
            first, second = values[:, 2 * pair], values[:, 2 * pair + 1]
            merged = (
                jnp.where(low, first, pltpu.roll(second, LANES // 2, 2)),
                jnp.where(low, pltpu.roll(first, LANES // 2, 2), second),
            )
            lanes = slice(pair * LANES, (pair + 1) * LANES)
            for part in range(2):
                rows = slice(part * half_depth, (part + 1) * half_depth)
                swapped = pltpu.roll(merged[part], 4, 1)
                swapped = jnp.where(real_row, -swapped, swapped)
                left[rows, lanes] = merged[part].reshape(half_depth, LANES).astype(jnp.bfloat16)
                right[rows, lanes] = swapped.reshape(half_depth, LANES).astype(jnp.bfloat16)
        out[channel, 0] = (
            lax.dot_general(left[...], left[...], TN, preferred_element_type=jnp.float32) * scale
        )
        out[channel, 1] = (
            lax.dot_general(left[...], right[...], TN, preferred_element_type=jnp.float32) * scale
        )


def visibilities(spectra, tm_count, inp_count, total_frames, inputs_all):
    devices, height, _ = spectra.shape
    per_device = CH // devices
    depth = 2 * tm_count * 8
    return pl.pallas_call(
        functools.partial(visibility_kernel, tm_count, inp_count, total_frames),
        grid=(height // 16,),
        in_specs=[pl.BlockSpec((devices, 16, LANES), lambda i: (0, i, 0))],
        out_specs=pl.BlockSpec((2, 2, inputs_all, inputs_all), lambda i: (i, 0, 0, 0)),
        out_shape=jax.ShapeDtypeStruct((per_device, 2, inputs_all, inputs_all), jnp.float32),
        scratch_shapes=[
            pltpu.VMEM((depth, inputs_all), jnp.bfloat16),
            pltpu.VMEM((depth, inputs_all), jnp.bfloat16),
        ],
        compiler_params=pltpu.CompilerParams(vmem_limit_bytes=50 * 2**20),
        name="visibilities",
    )(spectra)


def on_device(voltages, taps):
    in_dev, samples = voltages.shape
    frame_len = taps.shape[1]
    frames_dev = samples // frame_len
    tm_count, inp_count = lax.axis_size("tm"), lax.axis_size("inp")
    devices = tm_count * inp_count
    table = twiddles(frame_len)
    tail = frame_spectra(voltages, taps, table, True)
    tail, table, voltages = lax.optimization_barrier((tail, table, voltages))
    carried = lax.ppermute(tail, "tm", [(i, i + 1) for i in range(tm_count - 1)])
    main = frame_spectra(voltages, taps, table, False)
    spectra = (main + carried.astype(jnp.float32)).astype(jnp.bfloat16)
    spectra = spectra.reshape(devices, -1, LANES)
    spectra = lax.all_to_all(spectra, ("tm", "inp"), split_axis=0, concat_axis=0, tiled=True)
    return visibilities(spectra, tm_count, inp_count, tm_count * frames_dev, inp_count * in_dev)


def solution(mesh):
    return jax.shard_map(
        on_device,
        mesh=mesh,
        in_specs=(P("inp", "tm"), P()),
        out_specs=P(("tm", "inp"), None, None, None),
        check_vma=False,
    )
```

```python
import functools
import math

import jax
import jax.numpy as jnp
from jax import lax
from jax.experimental import pallas as pl
from jax.experimental.pallas import tpu as pltpu
from jax.sharding import PartitionSpec as P

CH = 512
START = 1024
RADIX = 8
LANES = 128
NT = (((1,), (1,)), ((), ()))
TN = (((0,), (0,)), ((), ()))
PAIRS = ((1, 7), (2, 6), (3, 5))
TABLE_PARTS = 4 + 6 * len(PAIRS)
EVEN_ORDER = (0, 1, 4, 6, 8, 10, 12, 14)
ODD_ORDER = (2, 3, 15, 13, 11, 9, 7, 5)


def unit_roots(phase, frame_len):
    angle = (phase % frame_len).astype(jnp.float32) * jnp.float32(2.0 * math.pi / frame_len)
    return jnp.cos(angle), -jnp.sin(angle)


def turned(first, second):
    return first[0] * second[0] - first[1] * second[1], first[1] * second[0] + first[0] * second[1]


def table_places(res):
    if res % 4 == 0:
        return ((res // 2, False),), ((res // 2 + 1, False),)
    for index, (lead, mirror) in enumerate(PAIRS):
        start = 4 + 6 * index
        if res == lead:
            return ((start, False), (start + 4, True)), ((start + 2, False),)
        if res == mirror:
            return ((start + 3, False),), ((start + 1, False), (start + 5, True))


def table_kernel(frame_len, out):
    _, rows, span = out.shape
    shape = (rows, LANES)
    channel = pl.program_id(0) * rows + lax.broadcasted_iota(jnp.int32, shape, 0)
    column = lax.broadcasted_iota(jnp.int32, shape, 1)
    fine = unit_roots(RADIX * channel * column, frame_len)
    advance = unit_roots(RADIX * LANES * channel, frame_len)
    residue = lax.broadcasted_iota(jnp.int32, (RADIX, LANES), 0)
    base = unit_roots((START + residue) * lax.broadcasted_iota(jnp.int32, (RADIX, LANES), 1), frame_len)
    for res in range(RADIX):
        value = turned(fine, tuple(part[res : res + 1, :] for part in base))
        angle = 2.0 * math.pi * (LANES * (START + res) % frame_len) / frame_len
        turn = turned(advance, (jnp.float32(math.cos(angle)), jnp.float32(-math.sin(angle))))
        places = table_places(res)
        for start in range(0, span, LANES):
            for which in range(2):
                entry = value[which].astype(jnp.bfloat16)
                for part, negated in places[which]:
                    out[part, :, start : start + LANES] = -entry if negated else entry
            value = turned(value, turn)


def twiddles(frame_len):
    span = frame_len // RADIX
    eighth = CH // RADIX
    rows = 16
    table = pl.pallas_call(
        functools.partial(table_kernel, frame_len),
        grid=(eighth // rows,),
        out_specs=pl.BlockSpec((TABLE_PARTS, rows, span), lambda i: (0, i, 0)),
        out_shape=jax.ShapeDtypeStruct((TABLE_PARTS, eighth, span), jnp.bfloat16),
        name="twiddles",
    )()
    return table.reshape(TABLE_PARTS * eighth, span)


def spectra_kernel(tail, frames, width, batch, samples, taps, source, out, parts, sums_ref, wide, table, arrived):
    step = pl.program_id(0)
    taps_count = taps.shape[1]
    groups, low = samples.shape[0], samples.shape[2]
    in_dev = groups * low
    made = taps_count - 1 if tail else frames
    columns = frames * in_dev

    @pl.when(step == 0)
    def _():
        sums_ref[...] = jnp.zeros_like(sums_ref)
        if tail:
            parts[...] = jnp.zeros_like(parts)

    chunk = pl.ds(pl.multiple_of(step // batch * batch * width, batch * width), batch * width)
    load = pltpu.make_async_copy(source.at[:, chunk], table, arrived)

    @pl.when(step % batch == 0)
    def _():
        load.start()

    base = step % batch * width
    for lane in range(width // LANES):
        lanes = slice(lane * LANES, (lane + 1) * LANES)
        places = pl.ds(pl.multiple_of(base + lane * LANES, LANES), LANES)
        for b in range(RADIX):
            for t in range(taps_count):
                wide[lane % 2, b, t] = jnp.broadcast_to(taps[b, t : t + 1, lanes], (low, LANES))
        for group in range(groups):
            kept = []
            for first in (0, 2, 1, 3):
                pair = []
                for b in (first, first + 4):
                    block = [samples[group, n * RADIX + b, :, lanes].astype(jnp.float32) for n in range(frames)]
                    totals = [None] * made
                    for t in range(taps_count):
                        weight = wide[lane % 2, b, t]
                        for m in range(made):
                            n = frames + m - t if tail else m - t
                            if 0 <= n < frames:
                                term = weight * block[n]
                                totals[m] = term if totals[m] is None else totals[m] + term
                    pair.append(totals)
                kept.append(([x + y for x, y in zip(*pair)], [x - y for x, y in zip(*pair)]))
            (s0, d0), (s2, d2), (s1, d1), (s3, d3) = kept
            root = jnp.float32(math.sqrt(0.5))
            for m in range(made):
                rows = slice(m * in_dev + group * low, m * in_dev + (group + 1) * low)
                even, odd = s0[m] + s2[m], s1[m] + s3[m]
                across, along = (d1[m] - d3[m]) * root, (d1[m] + d3[m]) * root
                parts[0, rows, places] = even + odd
                parts[1, rows, places] = even - odd
                parts[2, rows, places] = d0[m] + across
                parts[3, rows, places] = along + d2[m]
                parts[4, rows, places] = s0[m] - s2[m]
                parts[5, rows, places] = s1[m] - s3[m]
                parts[6, rows, places] = d0[m] - across
                parts[7, rows, places] = along - d2[m]

    eighth = table.shape[0] // TABLE_PARTS

    def product(first, last, part):
        rows = table[first * eighth : last * eighth, :]
        return lax.dot_general(rows, parts[part], NT, preferred_element_type=jnp.float32)

    @pl.when(step % batch == batch - 1)
    def _():
        load.wait()
        sums_ref[: 2 * eighth] += product(0, 2, 0)
        sums_ref[2 * eighth : 4 * eighth] += product(2, 4, 1)
        for index in range(len(PAIRS)):
            rows = slice((4 + 4 * index) * eighth, (8 + 4 * index) * eighth)
            first = 4 + 6 * index
            sums_ref[rows] += product(first, first + 4, 2 + 2 * index) + product(first + 2, first + 6, 3 + 2 * index)

    @pl.when(step == pl.num_programs(0) - 1)
    def _():
        scale = jnp.float32(1.0 / math.sqrt(RADIX * width * pl.num_programs(0)))
        tiles = columns // LANES
        height = 2 * RADIX * tiles
        for start in range(0, eighth, 8):
            both = []
            for order in (EVEN_ORDER, ODD_ORDER):
                pieces = [
                    sums_ref[part * eighth + start : part * eighth + start + 8, tile * LANES : (tile + 1) * LANES]
                    for part in order
                    for tile in range(tiles)
                ]
                both.append(jnp.transpose(jnp.stack(pieces), (1, 0, 2)) * scale)
            value = jnp.stack(both, axis=1).reshape(16, len(pieces), LANES)
            out[2 * start : 2 * start + 16] = value.astype(out.dtype)


def frame_spectra(voltages, taps, table, tail, width=256, batch=4):
    in_dev, length = voltages.shape
    tap_count, frame_len = taps.shape
    frames = length // frame_len
    span = frame_len // RADIX
    devices = CH // 4
    columns = frames * in_dev

    low = 8
    samples = voltages.reshape(in_dev // low, low, frames * RADIX, span)
    samples = jnp.transpose(samples, (0, 2, 1, 3))
    taps = jnp.transpose(taps.reshape(tap_count, RADIX, span), (1, 0, 2))
    in_specs = [
        pl.BlockSpec((in_dev // low, frames * RADIX, low, width), lambda i: (0, 0, 0, i)),
        pl.BlockSpec((RADIX, tap_count, width), lambda i: (0, 0, i)),
        pl.BlockSpec(memory_space=pl.ANY),
    ]
    height = 8 * (columns // LANES)
    return pl.pallas_call(
        functools.partial(spectra_kernel, tail, frames, width, batch),
        grid=(span // width,),
        in_specs=in_specs,
        out_specs=pl.BlockSpec((devices, height, LANES), lambda i: (0, 0, 0)),
        out_shape=jax.ShapeDtypeStruct((devices, height, LANES), jnp.bfloat16 if tail else jnp.float32),
        scratch_shapes=[
            pltpu.VMEM((RADIX, columns, batch * width), jnp.float32),
            pltpu.VMEM((2 * CH, columns), jnp.float32),
            pltpu.VMEM((2, RADIX, tap_count, low, LANES), jnp.float32),
            pltpu.VMEM((table.shape[0], batch * width), table.dtype),
            pltpu.SemaphoreType.DMA,
        ],
        compiler_params=pltpu.CompilerParams(vmem_limit_bytes=50 * 2**20),
        cost_estimate=pl.CostEstimate(
            flops=2 * columns * (7 * CH // 2) * span, bytes_accessed=26 * 2**20, transcendentals=0
        ),
        name="tail_spectra" if tail else "main_spectra",
    )(samples, taps, table)


def visibility_kernel(tm_count, inp_count, total_frames, block, out, left, right):
    lane = lax.broadcasted_iota(jnp.int32, (tm_count, 8, LANES), 2)
    row = lax.broadcasted_iota(jnp.int32, (tm_count, 8, LANES), 1)
    low = lane < LANES // 2
    real_row = row < 4
    half_depth = tm_count * 8
    scale = jnp.float32(1.0 / total_frames)
    for channel in range(block.shape[1] // 8):
        values = block[...].astype(jnp.float32)[:, channel * 8 : channel * 8 + 8, :]
        values = values.reshape(tm_count, inp_count, 8, LANES)
        for pair in range(inp_count // 2):
            first, second = values[:, 2 * pair], values[:, 2 * pair + 1]
            merged = (
                jnp.where(low, first, pltpu.roll(second, LANES // 2, 2)),
                jnp.where(low, pltpu.roll(first, LANES // 2, 2), second),
            )
            lanes = slice(pair * LANES, (pair + 1) * LANES)
            for part in range(2):
                rows = slice(part * half_depth, (part + 1) * half_depth)
                swapped = pltpu.roll(merged[part], 4, 1)
                swapped = jnp.where(real_row, -swapped, swapped)
                left[rows, lanes] = merged[part].reshape(half_depth, LANES).astype(jnp.bfloat16)
                right[rows, lanes] = swapped.reshape(half_depth, LANES).astype(jnp.bfloat16)
        out[channel, 0] = (
            lax.dot_general(left[...], left[...], TN, preferred_element_type=jnp.float32) * scale
        )
        out[channel, 1] = (
            lax.dot_general(left[...], right[...], TN, preferred_element_type=jnp.float32) * scale
        )


def visibilities(spectra, tm_count, inp_count, total_frames, inputs_all):
    devices, height, _ = spectra.shape
    per_device = CH // devices
    depth = 2 * tm_count * 8
    return pl.pallas_call(
        functools.partial(visibility_kernel, tm_count, inp_count, total_frames),
        grid=(height // 16,),
        in_specs=[pl.BlockSpec((devices, 16, LANES), lambda i: (0, i, 0))],
        out_specs=pl.BlockSpec((2, 2, inputs_all, inputs_all), lambda i: (i, 0, 0, 0)),
        out_shape=jax.ShapeDtypeStruct((per_device, 2, inputs_all, inputs_all), jnp.float32),
        scratch_shapes=[
            pltpu.VMEM((depth, inputs_all), jnp.bfloat16),
            pltpu.VMEM((depth, inputs_all), jnp.bfloat16),
        ],
        compiler_params=pltpu.CompilerParams(vmem_limit_bytes=50 * 2**20),
        name="visibilities",
    )(spectra)


def on_device(voltages, taps):
    in_dev, samples = voltages.shape
    frame_len = taps.shape[1]
    frames_dev = samples // frame_len
    tm_count, inp_count = lax.axis_size("tm"), lax.axis_size("inp")
    devices = tm_count * inp_count
    table = twiddles(frame_len)
    tail = frame_spectra(voltages, taps, table, True)
    tail, table, voltages = lax.optimization_barrier((tail, table, voltages))
    carried = lax.ppermute(tail, "tm", [(i, i + 1) for i in range(tm_count - 1)])
    main = frame_spectra(voltages, taps, table, False)
    spectra = (main + carried.astype(jnp.float32)).astype(jnp.bfloat16)
    spectra = spectra.reshape(devices, -1, LANES)
    spectra = lax.all_to_all(spectra, ("tm", "inp"), split_axis=0, concat_axis=0, tiled=True)
    return visibilities(spectra, tm_count, inp_count, tm_count * frames_dev, inp_count * in_dev)


def solution(mesh):
    return jax.shard_map(
        on_device,
        mesh=mesh,
        in_specs=(P("inp", "tm"), P()),
        out_specs=P(("tm", "inp"), None, None, None),
        check_vma=False,
    )
```
